256 devices in a mesh: row: 16 (over x, z_lo, core), col: 16 (over y, z_hi).
Axes of the slice: x: 4, y: 4, z: 8 (z_hi: 4, z_lo: 2; z = z_hi * 2 + z_lo), core: 2. Of those that a mesh axis runs over, the one named last changes fastest.
Arguments:
- tiles: float32 [16, 16, 128, 128, 128], P('row', 'col'), may hold values from -0.125 to 0.125
- tile_rows: int32 [16, 16, 128], P('row', 'col'), may hold values from 0 to 63, as said below
- tile_cols: int32 [16, 16, 128], P('row', 'col'), may hold values from 0 to 63, as said below
- tile_counts: int32 [16, 16], P('row', 'col'), may hold values from 1 to 128, as said below
- vectors: float32 [8, 131072], P(None, ('row', 'col')), may hold values from -6 to 6
Outputs:
- product: float32 [8, 131072], P(None, ('row', 'col'))
The draws below stay inside these ranges and needn't reach their ends.
Inputs may be any that keep to these rules, and one draw needn't show every extreme that they name: `tile_counts`: each device has 1 to 128 live slots; the target count of grid row r is the ceiling of 128 * (r + 1) / 16 less a jitter of 0 to 32, at least 1; one device of the last grid row has exactly 128. `tile_rows`: live slots of a device name distinct tiles on or below the block diagonal (global block row at least global block column); slots past the count hold 0. `tile_cols`: drawn together with tile_rows; slots past the count hold 0.
All inputs are finite; a program needn't handle non-finite values.
Results may differ from the reference program's by a relative error of at most 0.0003.
Values sent between devices are 32-bit elements; how exact they have to be, the bound alone decides.
No kernel may reach another device: no remote copies, remote signals or barrier semaphores. Data moves between devices by JAX's collectives and lax.ppermute only.
A program may use at most 64 MiB of HBM per device.

```python
import jax
import jax.numpy as jnp
from jax import lax

TILE = 128
VECS = 8
TILES_DEV = 128
BLOCKS_DEV = 4
ROW_BLOCKS = 64
COL_BLOCKS = 64
DIM = 131072
N_ROW = 16
N_COL = 16


def pattern(key):
    row_blocks = N_COL * BLOCKS_DEV
    col_blocks = N_ROW * BLOCKS_DEV
    cells = row_blocks * col_blocks
    cell = jnp.arange(cells, dtype=jnp.int32)
    local_row = cell // col_blocks
    local_col = cell % col_blocks
    devices = N_ROW * N_COL
    spread = max(2 ** 30 // cells, 2)

    def one(device, sub):
        grid_row = device // N_COL
        grid_col = device % N_COL
        big_row = grid_row * row_blocks + local_row
        big_col = (local_col // BLOCKS_DEV * N_COL + grid_col) * BLOCKS_DEV + local_col % BLOCKS_DEV
        lower = big_row >= big_col
        scores = jax.random.randint(sub, (cells,), 0, spread, dtype=jnp.int32) * cells + cell
        scores = jnp.where(lower, scores, -1 - cell)
        unused, picked = lax.top_k(scores, TILES_DEV)
        return (picked.astype(jnp.int32), jnp.sum(lower.astype(jnp.int32)))
    base_key = jax.random.fold_in(key, 11)
    keys = jax.random.split(base_key, devices)
    index = jnp.arange(devices, dtype=jnp.int32)
    picked, avail = jax.vmap(one)(index, keys)
    grid_row = index // N_COL
    grid_col = index % N_COL
    base = (TILES_DEV * (grid_row + 1) + N_ROW - 1) // N_ROW
    jitter = jax.random.randint(jax.random.fold_in(key, 12), (devices,), 0, TILES_DEV // 4 + 1, dtype=jnp.int32)
    target = jnp.maximum(base - jitter, 1)
    chosen = jax.random.randint(jax.random.fold_in(key, 13), (), 0, N_COL, dtype=jnp.int32)
    target = jnp.where((grid_row == N_ROW - 1) & (grid_col == chosen), TILES_DEV, target)
    count = jnp.minimum(target, avail).astype(jnp.int32)
    valid = jnp.arange(TILES_DEV, dtype=jnp.int32)[None, :] < count[:, None]
    rows = jnp.where(valid, picked // col_blocks, 0).astype(jnp.int32)
    cols = jnp.where(valid, picked % col_blocks, 0).astype(jnp.int32)
    return (rows.reshape(N_ROW, N_COL, TILES_DEV), cols.reshape(N_ROW, N_COL, TILES_DEV), count.reshape(N_ROW, N_COL))


def draw_tile_rows(key, part):
    return pattern(key)[0]


def draw_tile_cols(key, part):
    return pattern(key)[1]


def draw_tile_counts(key, part):
    return pattern(key)[2]


def block_levels(own_key, dims, cuts, least, largest):
    level, own = 1.0, jax.random.fold_in(own_key, 6)
    for position, parts in cuts:
        steps = jnp.exp(jax.random.uniform(jax.random.fold_in(own, position), (parts,), jnp.float32, least / len(cuts), largest / len(cuts)))
        level = level * jnp.repeat(steps, dims[position] // parts).reshape([-1 if axis == position else 1 for axis in range(len(dims))])
    return level


def noise(rng, extent, scale, reach, cuts=(), kind=jnp.bfloat16):
    result = scale * jax.random.normal(rng, extent, jnp.float32)
    if cuts:
        result = result * block_levels(rng, extent, cuts, -0.22, 0.18)
    return jnp.clip(result, -reach, reach).astype(kind)


def setup_inputs(seed: int = 0) -> dict:
    seeds = jax.random.split(jax.random.key(seed), 6)
    tiles = noise(seeds[0], (N_ROW, N_COL, TILES_DEV, TILE, TILE), (TILE * 16) ** -0.5, 0.125, ((0, 16), (1, 16)), jnp.float32)
    tile_rows = draw_tile_rows(jax.random.fold_in(seeds[5], 71), 0)
    tile_cols = draw_tile_cols(jax.random.fold_in(seeds[5], 71), 0)
    tile_counts = draw_tile_counts(jax.random.fold_in(seeds[5], 71), 0)
    vectors = noise(seeds[4], (VECS, DIM), 1.0, 6.0, ((1, 256),), jnp.float32)
    return {"tiles": tiles, "tile_rows": tile_rows, "tile_cols": tile_cols, "tile_counts": tile_counts, "vectors": vectors}


def device_terms(blocks, rows, cols, count, row_inputs, col_inputs):
    valid = jnp.arange(TILES_DEV, dtype=jnp.int32) < count
    from_cols = jnp.take(col_inputs, cols, axis=1)
    from_rows = jnp.take(row_inputs, rows, axis=1)
    first = jnp.einsum('tab,ktb->kta', blocks, from_cols, precision=lax.Precision.HIGHEST)
    second = jnp.einsum('tab,kta->ktb', blocks, from_rows, precision=lax.Precision.HIGHEST)
    row_hits = ((rows[:, None] == jnp.arange(ROW_BLOCKS, dtype=jnp.int32)[None, :]) & valid[:, None]).astype(blocks.dtype)
    col_hits = ((cols[:, None] == jnp.arange(COL_BLOCKS, dtype=jnp.int32)[None, :]) & valid[:, None]).astype(blocks.dtype)
    row_part = jnp.einsum('kta,ti->kia', first, row_hits, precision=lax.Precision.HIGHEST)
    col_part = jnp.einsum('ktb,tj->kjb', second, col_hits, precision=lax.Precision.HIGHEST)
    return row_part, col_part


def reference(tiles, tile_rows, tile_cols, tile_counts, vectors):
    grid = vectors.reshape(VECS, N_ROW, N_COL, BLOCKS_DEV, TILE)
    flat_tiles = tiles.reshape(N_ROW * N_COL, TILES_DEV, TILE, TILE)
    flat_rows = tile_rows.reshape(N_ROW * N_COL, TILES_DEV)
    flat_cols = tile_cols.reshape(N_ROW * N_COL, TILES_DEV)
    flat_counts = tile_counts.reshape(N_ROW * N_COL)

    def step(total, device):
        grid_row = device // N_COL
        grid_col = device % N_COL
        row_inputs = lax.dynamic_index_in_dim(grid, grid_row, 1, keepdims=False).reshape(VECS, ROW_BLOCKS, TILE)
        col_inputs = lax.dynamic_index_in_dim(grid, grid_col, 2, keepdims=False).reshape(VECS, COL_BLOCKS, TILE)
        blocks = lax.dynamic_index_in_dim(flat_tiles, device, 0, keepdims=False)
        rows = lax.dynamic_index_in_dim(flat_rows, device, 0, keepdims=False)
        cols = lax.dynamic_index_in_dim(flat_cols, device, 0, keepdims=False)
        count = lax.dynamic_index_in_dim(flat_counts, device, 0, keepdims=False)
        row_part, col_part = device_terms(blocks, rows, cols, count, row_inputs, col_inputs)
        total = total.at[:, grid_row].add(row_part.reshape(VECS, N_COL, BLOCKS_DEV, TILE))
        total = total.at[:, :, grid_col].add(col_part.reshape(VECS, N_ROW, BLOCKS_DEV, TILE))
        return total, None

    start = jnp.zeros((VECS, N_ROW, N_COL, BLOCKS_DEV, TILE), vectors.dtype)
    total, unused = lax.scan(step, start, jnp.arange(N_ROW * N_COL, dtype=jnp.int32))
    return total.reshape(VECS, DIM)
```

```python
import jax
import jax.numpy as jnp
from jax import lax
from jax.experimental import pallas as pl
from jax.experimental.pallas import tpu as pltpu
from jax.sharding import PartitionSpec as P

GROUP = 8


def split(value):
    high = value.astype(jnp.bfloat16)
    low = (value - high.astype(jnp.float32)).astype(jnp.bfloat16)
    return high, low


def tile_kernel(rows, cols, count, row_inputs, col_inputs, tiles, row_part, col_part,
                held, row_split, col_split, row_sum, col_sum, arrived):
    slots = held.shape[0]
    side = held.shape[1]
    groups = slots // GROUP
    blocks = row_inputs.shape[0]

    def fetch(group):
        place = pl.ds(group * GROUP, GROUP)
        return pltpu.make_async_copy(tiles.at[place], held.at[place], arrived.at[group])

    for group in range(groups):
        fetch(group).start()
    for source, target in ((row_inputs, row_split), (col_inputs, col_split)):
        high, low = split(source[...])
        target[...] = jnp.concatenate([high, low], axis=1)
    row_sum[...] = jnp.zeros_like(row_sum)
    col_sum[...] = jnp.zeros_like(col_sum)
    live = count[0]

    def step(group, carry):
        fetch(group).wait()
        results = []
        for offset in range(GROUP):
            slot = group * GROUP + offset
            row = rows[slot]
            col = cols[slot]
            high, low = split(held[slot])
            from_cols = col_split[col]
            from_rows = row_split[row]
            first = lax.dot_general(
                jnp.concatenate([from_cols, from_cols], axis=1),
                jnp.concatenate([high, low], axis=1),
                (((1,), (1,)), ((), ())),
                preferred_element_type=jnp.float32,
            )
            second = lax.dot_general(
                jnp.concatenate([from_rows, from_rows], axis=1),
                jnp.concatenate([high, low], axis=0),
                (((1,), (0,)), ((), ())),
                preferred_element_type=jnp.float32,
            )
            dead = slot >= live
            results.append((jnp.where(dead, blocks, row), jnp.where(dead, blocks, col),
                            first[:8] + first[8:], second[:8] + second[8:]))
        for row, col, first, second in results:
            row_sum[row] += first
            col_sum[col] += second
        return carry

    lax.fori_loop(0, groups, step, 0)
    row_part[...] = row_sum[:blocks]
    col_part[...] = col_sum[:blocks]


def multiply(tiles, rows, cols, count, row_inputs, col_inputs):
    slots, side, _ = tiles.shape
    blocks, vectors, _ = row_inputs.shape
    part = jax.ShapeDtypeStruct((blocks, vectors, side), jnp.float32)
    smem = pl.BlockSpec(memory_space=pltpu.SMEM)
    vmem = pl.BlockSpec(memory_space=pltpu.VMEM)
    return pl.pallas_call(
        tile_kernel,
        out_shape=(part, part),
        in_specs=[smem, smem, smem, vmem, vmem, pl.BlockSpec(memory_space=pl.ANY)],
        out_specs=(vmem, vmem),
        scratch_shapes=[
            pltpu.VMEM((slots, side, side), jnp.float32),
            pltpu.VMEM((blocks, 2 * vectors, side), jnp.bfloat16),
            pltpu.VMEM((blocks, 2 * vectors, side), jnp.bfloat16),
            pltpu.VMEM((blocks + 8, vectors, side), jnp.float32),
            pltpu.VMEM((blocks + 8, vectors, side), jnp.float32),
            pltpu.SemaphoreType.DMA((slots // GROUP,)),
        ],
        compiler_params=pltpu.CompilerParams(vmem_limit_bytes=20 * 1024 * 1024),
        cost_estimate=pl.CostEstimate(flops=4 * 16 * 256 * side * slots, bytes_accessed=4 * slots * side * side, transcendentals=0),
    )(rows, cols, count, row_inputs, col_inputs, tiles)


def body(tiles, tile_rows, tile_cols, tile_counts, vectors):
    vector_count, width = vectors.shape
    side = tiles.shape[-1]
    local_blocks = width // side
    row_devices = lax.axis_size("row")
    col_devices = lax.axis_size("col")
    own = vectors.reshape(vector_count, local_blocks, side).transpose(1, 0, 2)

    def gather(axis, devices):
        copies = jnp.broadcast_to(own[None], (devices, *own.shape)).reshape(-1, vector_count, side)
        return lax.all_to_all(copies, axis, 0, 0, tiled=True)

    col_inputs = gather("row", row_devices)
    row_inputs = gather("col", col_devices)
    row_part, col_part = multiply(tiles[0, 0], tile_rows[0, 0], tile_cols[0, 0], tile_counts[0], row_inputs, col_inputs)
    row_terms = lax.all_to_all(row_part, "col", 0, 0, tiled=True)
    col_terms = lax.all_to_all(col_part, "row", 0, 0, tiled=True)
    total = row_terms.reshape(col_devices, *own.shape).sum(0) + col_terms.reshape(row_devices, *own.shape).sum(0)
    return total.transpose(1, 0, 2).reshape(vector_count, width)


def solution(mesh):
    in_specs = (
        P("row", "col", None, None, None),
        P("row", "col", None),
        P("row", "col", None),
        P("row", "col"),
        P(None, ("row", "col")),
    )
    out_specs = P(None, ("row", "col"))
    return jax.shard_map(body, mesh=mesh, in_specs=in_specs, out_specs=out_specs, check_vma=False)
```

```python
import functools

import jax
import jax.numpy as jnp
from jax import lax
from jax.experimental import pallas as pl
from jax.experimental.pallas import tpu as pltpu
from jax.sharding import PartitionSpec as P

CHUNK = 16
AHEAD = 3
SLIM = 62
TLIM = 48
JOIN = 5 * 10 ** 10
FLOPS = 4 * 16 * 256 * 128 * 128
SMEM = pl.BlockSpec(memory_space=pltpu.SMEM)
VMEM = pl.BlockSpec(memory_space=pltpu.VMEM)
ANY = pl.BlockSpec(memory_space=pl.ANY)


def split(value):
    high = value.astype(jnp.bfloat16)
    low = (value - high.astype(jnp.float32)).astype(jnp.bfloat16)
    return high, low


def tile_kernel(inputs, outputs, *refs):
    places, tiles, row_source = refs[:3]
    col_sources = refs[3:3 + inputs]
    row_part = refs[3 + inputs]
    col_parts = refs[4 + inputs:4 + inputs + outputs]
    held, row_split, col_split, row_sum, col_sum, arrived = refs[4 + inputs + outputs:]
    slots = held.shape[0]
    chunks = slots // CHUNK
    vectors = row_sum.shape[1]

    def fetch(chunk):
        place = pl.ds(chunk * CHUNK, CHUNK)
        return pltpu.make_async_copy(tiles.at[place], held.at[place], arrived.at[chunk])

    for chunk in range(AHEAD):
        fetch(chunk).start()
    for sources, parts in (((row_source,), row_split), (col_sources, col_split)):
        start = 0
        for source in sources:
            high, low = split(source[...])
            parts[start:start + source.shape[0]] = jnp.concatenate([high, low], axis=1)
            start += source.shape[0]
        parts[start] = jnp.zeros_like(parts[start])
    row_sum[...] = jnp.zeros_like(row_sum)
    col_sum[...] = jnp.zeros_like(col_sum)

    def step(chunk, carry):
        fetch(chunk).wait()

        @pl.when(chunk + AHEAD < chunks)
        def _():
            fetch(chunk + AHEAD).start()

        results = []
        for offset in range(CHUNK):
            slot = chunk * CHUNK + offset
            place = places[slot]
            row, col = place // 128, place % 128
            high, low = split(held[slot])
            from_cols = col_split[col]
            from_rows = row_split[row]
            first = lax.dot_general(
                jnp.concatenate([from_cols, from_cols], axis=1),
                jnp.concatenate([high, low], axis=1),
                (((1,), (1,)), ((), ())), preferred_element_type=jnp.float32,
            )
            second = lax.dot_general(
                jnp.concatenate([from_rows, from_rows], axis=1),
                jnp.concatenate([high, low], axis=0),
                (((1,), (0,)), ((), ())), preferred_element_type=jnp.float32,
            )
            results.append((row, col, first[:vectors] + first[vectors:], second[:vectors] + second[vectors:]))
        for row, col, first, second in results:
            row_sum[row] += first
            col_sum[col] += second
        return carry

    lax.fori_loop(0, chunks, step, 0)
    row_part[...] = row_sum[:row_part.shape[0]]
    start = 0
    for part in col_parts:
        part[...] = col_sum[start:start + part.shape[0]]
        start += part.shape[0]


def multiply(places, tiles, row_input, col_inputs):
    slots, side, _ = tiles.shape
    row_blocks, vectors, _ = row_input.shape
    col_blocks = sum(part.shape[0] for part in col_inputs)
    parts = [jax.ShapeDtypeStruct(part.shape, jnp.float32) for part in [row_input, *col_inputs]]
    row_part, *col_parts = pl.pallas_call(
        functools.partial(tile_kernel, len(col_inputs), len(col_inputs)),
        out_shape=parts,
        in_specs=[SMEM, ANY, VMEM] + [VMEM] * len(col_inputs),
        out_specs=[VMEM] * len(parts),
        scratch_shapes=[
            pltpu.VMEM(tiles.shape, jnp.float32),
            pltpu.VMEM((row_blocks + 8, 2 * vectors, side), jnp.bfloat16),
            pltpu.VMEM((col_blocks + 8, 2 * vectors, side), jnp.bfloat16),
            pltpu.VMEM((row_blocks + 8, vectors, side), jnp.float32),
            pltpu.VMEM((col_blocks + 8, vectors, side), jnp.float32),
            pltpu.SemaphoreType.DMA((slots // CHUNK,)),
        ],
        compiler_params=pltpu.CompilerParams(vmem_limit_bytes=TLIM * 1024 * 1024),
        cost_estimate=pl.CostEstimate(flops=FLOPS, bytes_accessed=4 * slots * side * side, transcendentals=0),
    )(places, tiles, row_input, *col_inputs)
    return row_part, col_parts


def spread_kernel(own, out, local, arrived):
    fetch = pltpu.make_async_copy(own, local, arrived)
    fetch.start()
    fetch.wait()
    size = local.shape[0]
    value = local[...]
    for index in range(out.shape[0] // size):
        out[index * size:(index + 1) * size] = value


def spread(own, devices):
    return pl.pallas_call(
        spread_kernel,
        out_shape=[
            jax.ShapeDtypeStruct((devices * own.shape[0], *own.shape[1:]), own.dtype),
            jax.ShapeDtypeStruct(own.shape, own.dtype),
        ],
        in_specs=[ANY],
        out_specs=[VMEM, VMEM],
        scratch_shapes=[pltpu.SemaphoreType.DMA],
        compiler_params=pltpu.CompilerParams(vmem_limit_bytes=SLIM * 1024 * 1024),
    )(own)


def join_kernel(*refs):
    out = refs[-1]
    start = 0
    for part in refs[:-1]:
        out[start:start + part.shape[0]] = part[...]
        start += part.shape[0]


def join(parts):
    size = sum(part.shape[0] for part in parts)
    return pl.pallas_call(
        join_kernel,
        out_shape=jax.ShapeDtypeStruct((size, *parts[0].shape[1:]), parts[0].dtype),
        in_specs=[VMEM] * len(parts),
        out_specs=VMEM,
        compiler_params=pltpu.CompilerParams(vmem_limit_bytes=4 * 1024 * 1024),
        cost_estimate=pl.CostEstimate(flops=JOIN, bytes_accessed=1024, transcendentals=0),
    )(*parts)


def body(tiles, tile_rows, tile_cols, tile_counts, vectors):
    vector_count, width = vectors.shape
    slots, side = tiles.shape[2:4]
    local_blocks = width // side
    row_devices = lax.axis_size("row")
    col_devices = lax.axis_size("col")
    near = 4
    own = vectors.reshape(vector_count, local_blocks, side).transpose(1, 0, 2)

    def swap(value, offset):
        return lax.ppermute(value, "row", [(j, j ^ offset) for j in range(row_devices)])

    me = lax.axis_index("row")
    slot = jnp.arange(slots, dtype=jnp.int32)
    cols = tile_cols[0, 0]
    rel = ((cols // local_blocks) ^ me) * local_blocks + cols % local_blocks
    row_blocks = col_devices * local_blocks
    col_blocks = row_devices * local_blocks
    places = jnp.where(slot < tile_counts[0, 0], tile_rows[0, 0] * 128 + rel, row_blocks * 128 + col_blocks)

    copies, local = spread(own, col_devices)
    row_input = lax.all_to_all(copies, "col", 0, 0, tiled=True)
    close = join([local] + [swap(own, offset) for offset in range(1, near)])
    col_inputs = [close] + [swap(close, offset) for offset in range(near, row_devices, near)]
    row_part, col_parts = multiply(places, tiles[0, 0], row_input, col_inputs)
    row_terms = lax.all_to_all(row_part, "col", 0, 0, tiled=True)
    far = col_parts[0]
    for index in range(1, row_devices // near):
        far = far + swap(col_parts[index], index * near)
    far = far.reshape(near, local_blocks, vector_count, side)
    total = row_terms.reshape(col_devices, *own.shape).sum(0) + far[0]
    for offset in range(1, near):
        total = total + swap(far[offset], offset)
    return total.transpose(1, 0, 2).reshape(vector_count, width)


def solution(mesh):
    in_specs = (
        P("row", "col", None, None, None),
        P("row", "col", None),
        P("row", "col", None),
        P("row", "col"),
        P(None, ("row", "col")),
    )
    out_specs = P(None, ("row", "col"))
    return jax.shard_map(body, mesh=mesh, in_specs=in_specs, out_specs=out_specs, check_vma=False)
```

```python
import functools

import jax
import jax.numpy as jnp
from jax import lax
from jax.experimental import pallas as pl
from jax.experimental.pallas import tpu as pltpu
from jax.sharding import PartitionSpec as P

CHUNK = 32
AHEAD = 2
SLIM = 62
TLIM = 48
JOIN = 5 * 10 ** 10
ORDER = (2, 3, 1)
FLOPS = 4 * 16 * 256 * 128 * 128
SMEM = pl.BlockSpec(memory_space=pltpu.SMEM)
VMEM = pl.BlockSpec(memory_space=pltpu.VMEM)
ANY = pl.BlockSpec(memory_space=pl.ANY)


def split(value):
    high = value.astype(jnp.bfloat16)
    low = (value - high.astype(jnp.float32)).astype(jnp.bfloat16)
    return high, low


def take(refs, count):
    taken = refs[:count]
    del refs[:count]
    return taken


def tile_kernel(row_pieces, col_pieces, *refs):
    refs = list(refs)
    places, tiles = take(refs, 2)
    row_sources, col_sources = take(refs, row_pieces), take(refs, col_pieces)
    row_parts, col_parts = take(refs, row_pieces), take(refs, col_pieces)
    held, row_split, col_split, row_sum, col_sum, arrived = refs
    slots = held.shape[0]
    chunks = slots // CHUNK
    vectors = row_sum.shape[1]

    def fetch(chunk):
        place = pl.ds(chunk * CHUNK, CHUNK)
        return pltpu.make_async_copy(tiles.at[place], held.at[place], arrived.at[chunk])

    for chunk in range(AHEAD):
        fetch(chunk).start()
    for sources, parts in ((row_sources, row_split), (col_sources, col_split)):
        start = 0
        for source in sources:
            high, low = split(source[...])
            parts[start:start + source.shape[0]] = jnp.concatenate([high, low], axis=1)
            start += source.shape[0]
        parts[start] = jnp.zeros_like(parts[start])
    row_sum[...] = jnp.zeros_like(row_sum)
    col_sum[...] = jnp.zeros_like(col_sum)

    def step(chunk, carry):
        fetch(chunk).wait()

        @pl.when(chunk + AHEAD < chunks)
        def _():
            fetch(chunk + AHEAD).start()

        results = []
        for offset in range(CHUNK):
            slot = chunk * CHUNK + offset
            place = places[slot]
            row, col = place // 128, place % 128
            high, low = split(held[slot])
            from_cols = col_split[col]
            from_rows = row_split[row]
            first = lax.dot_general(
                jnp.concatenate([from_cols, from_cols], axis=1),
                jnp.concatenate([high, low], axis=1),
                (((1,), (1,)), ((), ())), preferred_element_type=jnp.float32,
            )
            second = lax.dot_general(
                jnp.concatenate([from_rows, from_rows], axis=1),
                jnp.concatenate([high, low], axis=0),
                (((1,), (0,)), ((), ())), preferred_element_type=jnp.float32,
            )
            results.append((row, col, first[:vectors] + first[vectors:], second[:vectors] + second[vectors:]))
        for row, col, first, second in results:
            row_sum[row] += first
            col_sum[col] += second
        return carry

    lax.fori_loop(0, chunks, step, 0)
    for parts, total in ((row_parts, row_sum), (col_parts, col_sum)):
        start = 0
        for part in parts:
            part[...] = total[start:start + part.shape[0]]
            start += part.shape[0]


def multiply(places, tiles, row_inputs, col_inputs):
    slots, side, _ = tiles.shape
    pieces = len(row_inputs), len(col_inputs)
    blocks = sum(part.shape[0] for part in row_inputs)
    vectors = row_inputs[0].shape[1]
    parts = [jax.ShapeDtypeStruct(part.shape, jnp.float32) for part in [*row_inputs, *col_inputs]]
    results = pl.pallas_call(
        functools.partial(tile_kernel, *pieces),
        out_shape=parts,
        in_specs=[SMEM, ANY] + [VMEM] * len(parts),
        out_specs=[VMEM] * len(parts),
        scratch_shapes=[
            pltpu.VMEM(tiles.shape, jnp.float32),
            pltpu.VMEM((blocks + 8, 2 * vectors, side), jnp.bfloat16),
            pltpu.VMEM((blocks + 8, 2 * vectors, side), jnp.bfloat16),
            pltpu.VMEM((blocks + 8, vectors, side), jnp.float32),
            pltpu.VMEM((blocks + 8, vectors, side), jnp.float32),
            pltpu.SemaphoreType.DMA((slots // CHUNK,)),
        ],
        compiler_params=pltpu.CompilerParams(vmem_limit_bytes=TLIM * 1024 * 1024),
        cost_estimate=pl.CostEstimate(flops=FLOPS, bytes_accessed=4 * slots * side * side, transcendentals=0),
    )(places, tiles, *row_inputs, *col_inputs)
    return results[:pieces[0]], results[pieces[0]:]


def join_kernel(*refs):
    out = refs[-1]
    start = 0
    for part in refs[:-1]:
        out[start:start + part.shape[0]] = part[...]
        start += part.shape[0]


def join(parts):
    size = sum(part.shape[0] for part in parts)
    return pl.pallas_call(
        join_kernel,
        out_shape=jax.ShapeDtypeStruct((size, *parts[0].shape[1:]), parts[0].dtype),
        in_specs=[VMEM] * len(parts),
        out_specs=VMEM,
        compiler_params=pltpu.CompilerParams(vmem_limit_bytes=4 * 1024 * 1024),
        cost_estimate=pl.CostEstimate(flops=JOIN, bytes_accessed=1024, transcendentals=0),
    )(*parts)


def fold_kernel(count, *refs):
    total = refs[0][...]
    for part in refs[1:count]:
        total = total + part[...]
    start = 0
    for out in refs[count:]:
        out[...] = total[start:start + out.shape[0]]
        start += out.shape[0]


def fold(parts, pieces):
    size, *rest = parts[0].shape
    out = jax.ShapeDtypeStruct((size // pieces, *rest), parts[0].dtype)
    return pl.pallas_call(
        functools.partial(fold_kernel, len(parts)),
        out_shape=[out] * pieces,
        in_specs=[VMEM] * len(parts),
        out_specs=[VMEM] * pieces,
        compiler_params=pltpu.CompilerParams(vmem_limit_bytes=4 * 1024 * 1024),
        cost_estimate=pl.CostEstimate(flops=JOIN, bytes_accessed=1024, transcendentals=0),
    )(*parts)


def body(tiles, tile_rows, tile_cols, tile_counts, vectors):
    vector_count, width = vectors.shape
    slots, side = tiles.shape[2:4]
    local_blocks = width // side
    row_devices = lax.axis_size("row")
    col_devices = lax.axis_size("col")
    own = vectors.reshape(vector_count, local_blocks, side).transpose(1, 0, 2)

    def swap(value, axis, offset):
        return lax.ppermute(value, axis, [(j, j ^ offset) for j in range(lax.axis_size(axis))])

    def swaps(values, axis, step):
        sent = {index: swap(values[index], axis, index * step) for index in ORDER}
        return [sent[index] for index in sorted(sent)]

    rows, cols = tile_rows[0, 0], tile_cols[0, 0]
    row_offset = (rows // local_blocks) ^ lax.axis_index("col")
    col_offset = (cols // local_blocks) ^ lax.axis_index("row")
    col_offset = (col_offset & 1) * (row_devices // 2) + (col_offset >> 1)
    places = (row_offset * local_blocks + rows % local_blocks) * 128 + col_offset * local_blocks + cols % local_blocks
    slot = jnp.arange(slots, dtype=jnp.int32)
    places = jnp.where(slot < tile_counts[0, 0], places, col_devices * local_blocks * 128 + row_devices * local_blocks)

    pair = join([own, swap(own, "row", 2)])
    close = join([own] + swaps([own] * 4, "col", 1))
    half = join([pair] + swaps([pair] * 4, "row", 4))
    row_inputs = [close] + swaps([close] * 4, "col", 4)
    col_inputs = [half, swap(half, "row", 1)]

    row_parts, col_parts = multiply(places, tiles[0, 0], row_inputs, col_inputs)

    half = fold([col_parts[0], swap(col_parts[1], "row", 1)], 4)
    close = fold([row_parts[0]] + swaps(row_parts, "col", 4), 4)
    pair = fold([half[0]] + swaps(half, "row", 4), 2)
    terms = [close[0]] + swaps(close, "col", 1) + [pair[0], swap(pair[1], "row", 2)]
    total = functools.reduce(jnp.add, terms)
    return total.transpose(1, 0, 2).reshape(vector_count, width)


def solution(mesh):
    in_specs = (
        P("row", "col", None, None, None),
        P("row", "col", None),
        P("row", "col", None),
        P("row", "col"),
        P(None, ("row", "col")),
    )
    out_specs = P(None, ("row", "col"))
    return jax.shard_map(body, mesh=mesh, in_specs=in_specs, out_specs=out_specs, check_vma=False)
```

```python
import functools

import jax
import jax.numpy as jnp
from jax import lax
from jax.experimental import pallas as pl
from jax.experimental.pallas import tpu as pltpu
from jax.sharding import PartitionSpec as P

CHUNK = 32
AHEAD = 2
SLIM = 62
TLIM = 24
JOIN = 5 * 10 ** 10
FETCH = True
RING = 8
PIECE = 16
PLIM = 24
PREP = 3 * 10 ** 10
FETCH_COST = 10 ** 10
ROW_JOIN = JOIN
FLOPS = 4 * 16 * 256 * 128 * 128
SMEM = pl.BlockSpec(memory_space=pltpu.SMEM)
VMEM = pl.BlockSpec(memory_space=pltpu.VMEM)
ANY = pl.BlockSpec(memory_space=pl.ANY)


def split(value):
    high = value.astype(jnp.bfloat16)
    low = (value - high.astype(jnp.float32)).astype(jnp.bfloat16)
    return high, low


def split_tiles_kernel(tiles, out, held, arrived):
    slots = out.shape[0]
    ring, size, side, _ = held.shape
    chunks = slots // size

    def fetch(chunk):
        return pltpu.make_async_copy(tiles.at[pl.ds(chunk * size, size)], held.at[chunk % ring], arrived.at[chunk % ring])

    for chunk in range(ring):
        fetch(chunk).start()

    def step(chunk, carry):
        fetch(chunk).wait()
        for offset in range(size):
            high, low = split(held[chunk % ring, offset])
            out[chunk * size + offset, :side, :] = high
            out[chunk * size + offset, side:, :] = low

        @pl.when(chunk + ring < chunks)
        def _():
            fetch(chunk + ring).start()

        return carry

    lax.fori_loop(0, chunks, step, 0)


def split_tiles(tiles):
    slots, side, _ = tiles.shape
    return pl.pallas_call(
        split_tiles_kernel,
        out_shape=jax.ShapeDtypeStruct((slots, 2 * side, side), jnp.bfloat16),
        in_specs=[ANY],
        out_specs=VMEM,
        scratch_shapes=[
            pltpu.VMEM((RING, PIECE, side, side), jnp.float32),
            pltpu.SemaphoreType.DMA((RING,)),
        ],
        compiler_params=pltpu.CompilerParams(vmem_limit_bytes=PLIM * 1024 * 1024),
        cost_estimate=pl.CostEstimate(flops=PREP, bytes_accessed=8 * slots * side * side, transcendentals=0),
    )(tiles)


def take(refs, count):
    taken = refs[:count]
    del refs[:count]
    return taken


def tile_kernel(row_pieces, col_pieces, *refs):
    refs = list(refs)
    places, tiles = take(refs, 2)
    row_sources, col_sources = take(refs, row_pieces), take(refs, col_pieces)
    row_parts, col_parts = take(refs, row_pieces), take(refs, col_pieces)
    row_split, col_split, row_sum, col_sum = refs
    slots, _, side = tiles.shape
    vectors = row_sum.shape[1]

    for sources, parts in ((row_sources, row_split), (col_sources, col_split)):
        start = 0
        for source in sources:
            high, low = split(source[...])
            parts[start:start + source.shape[0]] = jnp.concatenate([high, low], axis=1)
            start += source.shape[0]
        parts[start] = jnp.zeros_like(parts[start])
    row_sum[...] = jnp.zeros_like(row_sum)
    col_sum[...] = jnp.zeros_like(col_sum)

    def step(chunk, carry):
        results = []
        for offset in range(CHUNK):
            slot = chunk * CHUNK + offset
            place = places[slot]
            row, col = place // 128, place % 128
            pair = tiles[slot]
            from_cols = col_split[col]
            from_rows = row_split[row]
            first = lax.dot_general(
                jnp.concatenate([from_cols, from_cols], axis=1),
                jnp.concatenate([pair[:side], pair[side:]], axis=1),
                (((1,), (1,)), ((), ())), preferred_element_type=jnp.float32,
            )
            second = lax.dot_general(
                jnp.concatenate([from_rows, from_rows], axis=1),
                pair,
                (((1,), (0,)), ((), ())), preferred_element_type=jnp.float32,
            )
            results.append((row, col, first[:vectors] + first[vectors:], second[:vectors] + second[vectors:]))
        for row, col, first, second in results:
            row_sum[row] += first
            col_sum[col] += second
        return carry

    lax.fori_loop(0, slots // CHUNK, step, 0)
    for parts, total in ((row_parts, row_sum), (col_parts, col_sum)):
        start = 0
        for part in parts:
            part[...] = total[start:start + part.shape[0]]
            start += part.shape[0]


def multiply(places, tiles, row_inputs, col_inputs):
    slots, _, side = tiles.shape
    pieces = len(row_inputs), len(col_inputs)
    blocks = sum(part.shape[0] for part in row_inputs)
    vectors = row_inputs[0].shape[1]
    parts = [jax.ShapeDtypeStruct(part.shape, jnp.float32) for part in [*row_inputs, *col_inputs]]
    results = pl.pallas_call(
        functools.partial(tile_kernel, *pieces),
        out_shape=parts,
        in_specs=[SMEM] + [VMEM] * (1 + len(parts)),
        out_specs=[VMEM] * len(parts),
        scratch_shapes=[
            pltpu.VMEM((blocks + 8, 2 * vectors, side), jnp.bfloat16),
            pltpu.VMEM((blocks + 8, 2 * vectors, side), jnp.bfloat16),
            pltpu.VMEM((blocks + 8, vectors, side), jnp.float32),
            pltpu.VMEM((blocks + 8, vectors, side), jnp.float32),
        ],
        compiler_params=pltpu.CompilerParams(vmem_limit_bytes=TLIM * 1024 * 1024),
        cost_estimate=pl.CostEstimate(flops=FLOPS, bytes_accessed=4 * slots * side * side, transcendentals=0),
    )(places, tiles, *row_inputs, *col_inputs)
    return results[:pieces[0]], results[pieces[0]:]


def fetch_kernel(value, out):
    out[...] = value[...]


def fetch(value):
    return pl.pallas_call(
        fetch_kernel,
        out_shape=jax.ShapeDtypeStruct(value.shape, value.dtype),
        in_specs=[VMEM],
        out_specs=VMEM,
        compiler_params=pltpu.CompilerParams(vmem_limit_bytes=4 * 1024 * 1024),
        cost_estimate=pl.CostEstimate(flops=FETCH_COST, bytes_accessed=1024, transcendentals=0),
    )(value)


def join_kernel(*refs):
    out = refs[-1]
    start = 0
    for part in refs[:-1]:
        out[start:start + part.shape[0]] = part[...]
        start += part.shape[0]


def join(parts, cost=JOIN):
    size = sum(part.shape[0] for part in parts)
    return pl.pallas_call(
        join_kernel,
        out_shape=jax.ShapeDtypeStruct((size, *parts[0].shape[1:]), parts[0].dtype),
        in_specs=[VMEM] * len(parts),
        out_specs=VMEM,
        compiler_params=pltpu.CompilerParams(vmem_limit_bytes=4 * 1024 * 1024),
        cost_estimate=pl.CostEstimate(flops=cost, bytes_accessed=1024, transcendentals=0),
    )(*parts)


def fold_kernel(count, *refs):
    total = refs[0][...]
    for part in refs[1:count]:
        total = total + part[...]
    start = 0
    for out in refs[count:]:
        out[...] = total[start:start + out.shape[0]]
        start += out.shape[0]


def fold(parts, pieces):
    size, *rest = parts[0].shape
    out = jax.ShapeDtypeStruct((size // pieces, *rest), parts[0].dtype)
    return pl.pallas_call(
        functools.partial(fold_kernel, len(parts)),
        out_shape=[out] * pieces,
        in_specs=[VMEM] * len(parts),
        out_specs=[VMEM] * pieces,
        compiler_params=pltpu.CompilerParams(vmem_limit_bytes=4 * 1024 * 1024),
        cost_estimate=pl.CostEstimate(flops=JOIN, bytes_accessed=1024, transcendentals=0),
    )(*parts)


def body(tiles, tile_rows, tile_cols, tile_counts, vectors):
    vector_count, width = vectors.shape
    slots, side = tiles.shape[2:4]
    local_blocks = width // side
    row_devices = lax.axis_size("row")
    col_devices = lax.axis_size("col")
    own = vectors.reshape(vector_count, local_blocks, side).transpose(1, 0, 2)

    def swap(value, axis, offset):
        return lax.ppermute(value, axis, [(j, j ^ offset) for j in range(lax.axis_size(axis))])

    def gray(offset):
        return offset ^ (offset >> 1)

    rows, cols = tile_rows[0, 0], tile_cols[0, 0]
    row_offset = (rows // local_blocks) ^ lax.axis_index("col")
    col_offset = (cols // local_blocks) ^ lax.axis_index("row")
    row_offset = (row_offset & 12) + gray(row_offset & 3)
    near_z, near_x = col_offset >> 1 & 1, gray(col_offset >> 2)
    col_offset = (col_offset & 1 ^ near_z ^ near_x & 1 ^ near_x >> 1) * 8 + near_x * 2 + near_z
    places = (row_offset * local_blocks + rows % local_blocks) * 128 + col_offset * local_blocks + cols % local_blocks
    slot = jnp.arange(slots, dtype=jnp.int32)
    places = jnp.where(slot < tile_counts[0, 0], places, col_devices * local_blocks * 128 + row_devices * local_blocks)

    local = fetch(own) if FETCH else own
    couple = join([local, swap(own, "col", 1)])
    pair = join([local, swap(own, "row", 3)], ROW_JOIN)
    close = join([couple, swap(couple, "col", 3)])
    quad = join([pair, swap(pair, "row", 5)], ROW_JOIN)
    close, blocks = lax.optimization_barrier((close, tiles))
    pairs = split_tiles(blocks[0, 0])
    row_inputs = [close] + [swap(close, "col", offset) for offset in (4, 8, 12)]
    half = join([quad, swap(quad, "row", 13)], ROW_JOIN)
    col_inputs = [half, swap(half, "row", 1)]

    row_parts, col_parts = multiply(places, pairs, row_inputs, col_inputs)

    close = fold([row_parts[0]] + [swap(row_parts[index], "col", 4 * index) for index in (2, 1, 3)], 2)
    half = fold([col_parts[0], swap(col_parts[1], "row", 1)], 2)
    quad = fold([half[0], swap(half[1], "row", 13)], 2)
    couple = fold([close[0], swap(close[1], "col", 3)], 2)
    pair = fold([quad[0], swap(quad[1], "row", 5)], 2)
    terms = [couple[0], swap(couple[1], "col", 1), pair[0], swap(pair[1], "row", 3)]
    total = functools.reduce(jnp.add, terms)
    return total.transpose(1, 0, 2).reshape(vector_count, width)


def solution(mesh):
    in_specs = (
        P("row", "col", None, None, None),
        P("row", "col", None),
        P("row", "col", None),
        P("row", "col"),
        P(None, ("row", "col")),
    )
    out_specs = P(None, ("row", "col"))
    return jax.shard_map(body, mesh=mesh, in_specs=in_specs, out_specs=out_specs, check_vma=False)
```

```python
import functools

import jax
import jax.numpy as jnp
from jax import lax
from jax.experimental import pallas as pl
from jax.experimental.pallas import tpu as pltpu
from jax.sharding import PartitionSpec as P

CHUNK = 128
AHEAD = 2
SLIM = 62
TLIM = 24
JOIN = 5 * 10 ** 10
FETCH = True
RING = 4
PIECE = 16
PREP_RING = 8
PLIM = 24
PREP = 3 * 10 ** 10
FETCH_COST = 10 ** 10
ROW_JOIN = JOIN
ROW_FOLD = JOIN
FLOPS = 2 * 10 ** 10
SMEM = pl.BlockSpec(memory_space=pltpu.SMEM)
VMEM = pl.BlockSpec(memory_space=pltpu.VMEM)
ANY = pl.BlockSpec(memory_space=pl.ANY)


def split(value):
    high = value.astype(jnp.bfloat16)
    low = (value - high.astype(jnp.float32)).astype(jnp.bfloat16)
    return high, low


def split_tiles_kernel(tiles, out, held, arrived):
    slots = out.shape[0]
    ring, size, side, _ = held.shape
    chunks = slots // size

    def fetch(chunk):
        return pltpu.make_async_copy(tiles.at[pl.ds(chunk * size, size)], held.at[chunk % ring], arrived.at[chunk % ring])

    for chunk in range(ring):
        fetch(chunk).start()

    def step(chunk, carry):
        fetch(chunk).wait()
        for offset in range(size):
            high, low = split(held[chunk % ring, offset])
            out[chunk * size + offset, :side, :] = high
            out[chunk * size + offset, side:, :] = low

        @pl.when(chunk + ring < chunks)
        def _():
            fetch(chunk + ring).start()

        return carry

    lax.fori_loop(0, chunks, step, 0)


def split_tiles(tiles):
    slots, side, _ = tiles.shape
    return pl.pallas_call(
        split_tiles_kernel,
        out_shape=jax.ShapeDtypeStruct((slots, 2 * side, side), jnp.bfloat16),
        in_specs=[ANY],
        out_specs=VMEM,
        scratch_shapes=[
            pltpu.VMEM((PREP_RING, PIECE, side, side), jnp.float32),
            pltpu.SemaphoreType.DMA((PREP_RING,)),
        ],
        compiler_params=pltpu.CompilerParams(vmem_limit_bytes=PLIM * 1024 * 1024),
        cost_estimate=pl.CostEstimate(flops=PREP, bytes_accessed=8 * slots * side * side, transcendentals=0),
    )(tiles)


def take(refs, count):
    taken = refs[:count]
    del refs[:count]
    return taken


def product_kernel(flipped, pieces, outputs, *refs):
    refs = list(refs)
    places, pairs = take(refs, 2)
    sources, parts = take(refs, pieces), take(refs, outputs)
    inputs, sums = refs
    slots, _, side = pairs.shape
    vectors = sums.shape[1]
    start = 0
    for source in sources:
        high, low = split(source[...])
        inputs[start:start + source.shape[0]] = jnp.concatenate([high, low], axis=1)
        start += source.shape[0]
    inputs[start] = jnp.zeros_like(inputs[start])
    sums[...] = jnp.zeros_like(sums)

    def step(chunk, carry):
        results = []
        for offset in range(CHUNK):
            slot = chunk * CHUNK + offset
            place = places[slot]
            row, col = place // 128, place % 128
            pair = pairs[slot]
            if flipped:
                value, target, contract = inputs[row], col, 0
            else:
                value, target, contract = inputs[col], row, 1
                pair = jnp.concatenate([pair[:side], pair[side:]], axis=1)
            result = lax.dot_general(
                jnp.concatenate([value, value], axis=1), pair,
                (((1,), (contract,)), ((), ())), preferred_element_type=jnp.float32,
            )
            results.append((target, result[:vectors] + result[vectors:]))
        for target, result in results:
            sums[target] += result
        return carry

    lax.fori_loop(0, slots // CHUNK, step, 0)
    start = 0
    for part in parts:
        part[...] = sums[start:start + part.shape[0]]
        start += part.shape[0]


def product(flipped, places, pairs, sources, sizes):
    slots, _, side = pairs.shape
    blocks = sum(source.shape[0] for source in sources)
    vectors = sources[0].shape[1]
    return pl.pallas_call(
        functools.partial(product_kernel, flipped, len(sources), len(sizes)),
        out_shape=[jax.ShapeDtypeStruct((size, vectors, side), jnp.float32) for size in sizes],
        in_specs=[SMEM] + [VMEM] * (1 + len(sources)),
        out_specs=[VMEM] * len(sizes),
        scratch_shapes=[
            pltpu.VMEM((blocks + 8, 2 * vectors, side), jnp.bfloat16),
            pltpu.VMEM((sum(sizes) + 8, vectors, side), jnp.float32),
        ],
        compiler_params=pltpu.CompilerParams(vmem_limit_bytes=TLIM * 1024 * 1024),
        cost_estimate=pl.CostEstimate(flops=FLOPS, bytes_accessed=4 * slots * side * side, transcendentals=0),
    )(places, pairs, *sources)


def fetch_kernel(value, out):
    out[...] = value[...]


def fetch(value):
    return pl.pallas_call(
        fetch_kernel,
        out_shape=jax.ShapeDtypeStruct(value.shape, value.dtype),
        in_specs=[VMEM],
        out_specs=VMEM,
        compiler_params=pltpu.CompilerParams(vmem_limit_bytes=4 * 1024 * 1024),
        cost_estimate=pl.CostEstimate(flops=FETCH_COST, bytes_accessed=1024, transcendentals=0),
    )(value)


def join_kernel(*refs):
    out = refs[-1]
    start = 0
    for part in refs[:-1]:
        out[start:start + part.shape[0]] = part[...]
        start += part.shape[0]


def join(parts, cost=JOIN):
    size = sum(part.shape[0] for part in parts)
    return pl.pallas_call(
        join_kernel,
        out_shape=jax.ShapeDtypeStruct((size, *parts[0].shape[1:]), parts[0].dtype),
        in_specs=[VMEM] * len(parts),
        out_specs=VMEM,
        compiler_params=pltpu.CompilerParams(vmem_limit_bytes=4 * 1024 * 1024),
        cost_estimate=pl.CostEstimate(flops=cost, bytes_accessed=1024, transcendentals=0),
    )(*parts)


def fold_kernel(count, *refs):
    total = refs[0][...]
    for part in refs[1:count]:
        total = total + part[...]
    start = 0
    for out in refs[count:]:
        out[...] = total[start:start + out.shape[0]]
        start += out.shape[0]


def fold(parts, pieces, cost=JOIN):
    size, *rest = parts[0].shape
    out = jax.ShapeDtypeStruct((size // pieces, *rest), parts[0].dtype)
    return pl.pallas_call(
        functools.partial(fold_kernel, len(parts)),
        out_shape=[out] * pieces,
        in_specs=[VMEM] * len(parts),
        out_specs=[VMEM] * pieces,
        compiler_params=pltpu.CompilerParams(vmem_limit_bytes=4 * 1024 * 1024),
        cost_estimate=pl.CostEstimate(flops=cost, bytes_accessed=1024, transcendentals=0),
    )(*parts)


def body(tiles, tile_rows, tile_cols, tile_counts, vectors):
    vector_count, width = vectors.shape
    slots, side = tiles.shape[2:4]
    local_blocks = width // side
    row_devices = lax.axis_size("row")
    col_devices = lax.axis_size("col")
    own = vectors.reshape(vector_count, local_blocks, side).transpose(1, 0, 2)

    def swap(value, axis, offset):
        return lax.ppermute(value, axis, [(j, j ^ offset) for j in range(lax.axis_size(axis))])

    def gray(offset):
        return offset ^ (offset >> 1)

    rows, cols = tile_rows[0, 0], tile_cols[0, 0]
    row_offset = (rows // local_blocks) ^ lax.axis_index("col")
    col_offset = (cols // local_blocks) ^ lax.axis_index("row")
    row_offset = (row_offset & 12) + gray(row_offset & 3)
    near_z, near_x = col_offset >> 1 & 1, gray(col_offset >> 2)
    col_offset = (col_offset & 1 ^ near_z ^ near_x & 1 ^ near_x >> 1) * 8 + near_x * 2 + near_z
    places = (row_offset * local_blocks + rows % local_blocks) * 128 + col_offset * local_blocks + cols % local_blocks
    slot = jnp.arange(slots, dtype=jnp.int32)
    places = jnp.where(slot < tile_counts[0, 0], places, col_devices * local_blocks * 128 + row_devices * local_blocks)

    local = fetch(own) if FETCH else own
    couple = join([local, swap(own, "col", 1)])
    pair = join([local, swap(own, "row", 3)], ROW_JOIN)
    close = join([couple, swap(couple, "col", 3)])
    quad = join([pair, swap(pair, "row", 5)], ROW_JOIN)
    close, blocks = lax.optimization_barrier((close, tiles))
    pairs = split_tiles(blocks[0, 0])
    row_inputs = [close] + [swap(close, "col", offset) for offset in (4, 8, 12)]
    half = join([quad, swap(quad, "row", 13)], ROW_JOIN)
    col_inputs = [half, swap(half, "row", 1)]

    quarter, half_size = close.shape[0], half.shape[0]
    row_parts = product(False, places, pairs, col_inputs, [quarter] * RING)
    later_places, _ = lax.optimization_barrier((places, row_parts[0]))
    col_parts = product(True, later_places, pairs, row_inputs, [half_size] * 2)

    across = fold([row_parts[0], swap(row_parts[2], "col", 8)], 1)
    close = fold([across[0], swap(row_parts[1], "col", 4), swap(row_parts[3], "col", 12)], 2)
    half = fold([col_parts[0], swap(col_parts[1], "row", 1)], 2, ROW_FOLD)
    quad = fold([half[0], swap(half[1], "row", 13)], 2, ROW_FOLD)
    couple = fold([close[0], swap(close[1], "col", 3)], 2)
    pair = fold([quad[0], swap(quad[1], "row", 5)], 2, ROW_FOLD)
    terms = [couple[0], swap(couple[1], "col", 1), pair[0], swap(pair[1], "row", 3)]
    total = functools.reduce(jnp.add, terms)
    return total.transpose(1, 0, 2).reshape(vector_count, width)


def solution(mesh):
    in_specs = (
        P("row", "col", None, None, None),
        P("row", "col", None),
        P("row", "col", None),
        P("row", "col"),
        P(None, ("row", "col")),
    )
    out_specs = P(None, ("row", "col"))
    return jax.shard_map(body, mesh=mesh, in_specs=in_specs, out_specs=out_specs, check_vma=False)
```

```python
import functools

import jax
import jax.numpy as jnp
from jax import lax
from jax.experimental import pallas as pl
from jax.experimental.pallas import tpu as pltpu
from jax.sharding import PartitionSpec as P

CHUNK = 128
AHEAD = 2
SLIM = 62
TLIM = 24
JOIN = 5 * 10 ** 10
FETCH = True
RING = 4
PIECE = 8
PREP_RING = 2
HEAD = 16
PLIM = 24
PREP = 3 * 10 ** 10
FETCH_COST = 10 ** 10
ROW_JOIN = JOIN
ROW_FOLD = JOIN
FLOPS = 2 * 10 ** 10
SMEM = pl.BlockSpec(memory_space=pltpu.SMEM)
VMEM = pl.BlockSpec(memory_space=pltpu.VMEM)
ANY = pl.BlockSpec(memory_space=pl.ANY)


def split(value):
    high = value.astype(jnp.bfloat16)
    low = (value - high.astype(jnp.float32)).astype(jnp.bfloat16)
    return high, low


def split_tiles_kernel(tiles, out, held, arrived):
    slots = out.shape[0]
    ring, size, side, _ = held.shape
    chunks = slots // size

    def fetch(chunk):
        return pltpu.make_async_copy(tiles.at[pl.ds(chunk * size, size)], held.at[chunk % ring], arrived.at[chunk % ring])

    for chunk in range(ring):
        fetch(chunk).start()

    def step(chunk, carry):
        fetch(chunk).wait()
        for offset in range(size):
            high, low = split(held[chunk % ring, offset])
            out[chunk * size + offset, :side, :] = high
            out[chunk * size + offset, side:, :] = low

        @pl.when(chunk + ring < chunks)
        def _():
            fetch(chunk + ring).start()

        return carry

    lax.fori_loop(0, chunks, step, 0)


def split_tiles(tiles):
    side = tiles.shape[1]
    return pl.pallas_call(
        split_tiles_kernel,
        out_shape=jax.ShapeDtypeStruct((HEAD, 2 * side, side), jnp.bfloat16),
        in_specs=[ANY],
        out_specs=VMEM,
        scratch_shapes=[
            pltpu.VMEM((PREP_RING, PIECE, side, side), jnp.float32),
            pltpu.SemaphoreType.DMA((PREP_RING,)),
        ],
        compiler_params=pltpu.CompilerParams(vmem_limit_bytes=PLIM * 1024 * 1024),
        cost_estimate=pl.CostEstimate(flops=PREP, bytes_accessed=1 << 24, transcendentals=0),
    )(tiles)


def take(refs, count):
    taken = refs[:count]
    del refs[:count]
    return taken


def product_kernel(flipped, pieces, outputs, *refs):
    refs = list(refs)
    places, tiles, pairs = take(refs, 3)
    sources, parts = take(refs, pieces), take(refs, outputs)
    inputs, sums = refs
    slots, side, _ = tiles.shape
    vectors = sums.shape[1]
    start = 0
    for source in sources:
        high, low = split(source[...])
        inputs[start:start + source.shape[0]] = jnp.concatenate([high, low], axis=1)
        start += source.shape[0]
    inputs[start] = jnp.zeros_like(inputs[start])
    sums[...] = jnp.zeros_like(sums)

    def step(chunk, carry):
        results = []
        for offset in range(CHUNK):
            slot = chunk * CHUNK + offset
            place = places[slot]
            row, col = place // 128, place % 128
            if offset < HEAD:
                high, low = pairs[slot, :side, :], pairs[slot, side:, :]
            else:
                high, low = split(tiles[slot])
            if flipped:
                value, target, contract = inputs[row], col, 0
            else:
                value, target, contract = inputs[col], row, 1
            pair = jnp.concatenate([high, low], axis=contract)
            result = lax.dot_general(
                jnp.concatenate([value, value], axis=1), pair,
                (((1,), (contract,)), ((), ())), preferred_element_type=jnp.float32,
            )
            results.append((target, result[:vectors] + result[vectors:]))
        for target, result in results:
            sums[target] += result
        return carry

    lax.fori_loop(0, slots // CHUNK, step, 0)
    start = 0
    for part in parts:
        part[...] = sums[start:start + part.shape[0]]
        start += part.shape[0]


def product(flipped, places, tiles, pairs, sources, sizes):
    slots, side, _ = tiles.shape
    blocks = sum(source.shape[0] for source in sources)
    vectors = sources[0].shape[1]
    return pl.pallas_call(
        functools.partial(product_kernel, flipped, len(sources), len(sizes)),
        out_shape=[jax.ShapeDtypeStruct((size, vectors, side), jnp.float32) for size in sizes],
        in_specs=[SMEM] + [VMEM] * (2 + len(sources)),
        out_specs=[VMEM] * len(sizes),
        scratch_shapes=[
            pltpu.VMEM((blocks + 8, 2 * vectors, side), jnp.bfloat16),
            pltpu.VMEM((sum(sizes) + 8, vectors, side), jnp.float32),
        ],
        compiler_params=pltpu.CompilerParams(vmem_limit_bytes=TLIM * 1024 * 1024),
        cost_estimate=pl.CostEstimate(flops=FLOPS, bytes_accessed=4 * slots * side * side, transcendentals=0),
    )(places, tiles, pairs, *sources)


def fetch_kernel(value, out):
    out[...] = value[...]


def fetch(value):
    return pl.pallas_call(
        fetch_kernel,
        out_shape=jax.ShapeDtypeStruct(value.shape, value.dtype),
        in_specs=[VMEM],
        out_specs=VMEM,
        compiler_params=pltpu.CompilerParams(vmem_limit_bytes=4 * 1024 * 1024),
        cost_estimate=pl.CostEstimate(flops=FETCH_COST, bytes_accessed=1024, transcendentals=0),
    )(value)


def join_kernel(*refs):
    out = refs[-1]
    start = 0
    for part in refs[:-1]:
        out[start:start + part.shape[0]] = part[...]
        start += part.shape[0]


def join(parts, cost=JOIN):
    size = sum(part.shape[0] for part in parts)
    return pl.pallas_call(
        join_kernel,
        out_shape=jax.ShapeDtypeStruct((size, *parts[0].shape[1:]), parts[0].dtype),
        in_specs=[VMEM] * len(parts),
        out_specs=VMEM,
        compiler_params=pltpu.CompilerParams(vmem_limit_bytes=4 * 1024 * 1024),
        cost_estimate=pl.CostEstimate(flops=cost, bytes_accessed=1024, transcendentals=0),
    )(*parts)


def fold_kernel(count, *refs):
    total = refs[0][...]
    for part in refs[1:count]:
        total = total + part[...]
    start = 0
    for out in refs[count:]:
        out[...] = total[start:start + out.shape[0]]
        start += out.shape[0]


def fold(parts, pieces, cost=JOIN):
    size, *rest = parts[0].shape
    out = jax.ShapeDtypeStruct((size // pieces, *rest), parts[0].dtype)
    return pl.pallas_call(
        functools.partial(fold_kernel, len(parts)),
        out_shape=[out] * pieces,
        in_specs=[VMEM] * len(parts),
        out_specs=[VMEM] * pieces,
        compiler_params=pltpu.CompilerParams(vmem_limit_bytes=4 * 1024 * 1024),
        cost_estimate=pl.CostEstimate(flops=cost, bytes_accessed=1024, transcendentals=0),
    )(*parts)


def body(tiles, tile_rows, tile_cols, tile_counts, vectors):
    vector_count, width = vectors.shape
    slots, side = tiles.shape[2:4]
    local_blocks = width // side
    row_devices = lax.axis_size("row")
    col_devices = lax.axis_size("col")
    own = vectors.reshape(vector_count, local_blocks, side).transpose(1, 0, 2)

    def swap(value, axis, offset):
        return lax.ppermute(value, axis, [(j, j ^ offset) for j in range(lax.axis_size(axis))])

    def gray(offset):
        return offset ^ (offset >> 1)

    rows, cols = tile_rows[0, 0], tile_cols[0, 0]
    row_offset = (rows // local_blocks) ^ lax.axis_index("col")
    col_offset = (cols // local_blocks) ^ lax.axis_index("row")
    row_offset = (row_offset & 12) + gray(row_offset & 3)
    near_z, near_x = col_offset >> 1 & 1, gray(col_offset >> 2)
    col_offset = (col_offset & 1 ^ near_z ^ near_x & 1 ^ near_x >> 1) * 8 + near_x * 2 + near_z
    places = (row_offset * local_blocks + rows % local_blocks) * 128 + col_offset * local_blocks + cols % local_blocks
    slot = jnp.arange(slots, dtype=jnp.int32)
    places = jnp.where(slot < tile_counts[0, 0], places, col_devices * local_blocks * 128 + row_devices * local_blocks)

    local = fetch(own) if FETCH else own
    couple = join([local, swap(own, "col", 1)])
    pair = join([local, swap(own, "row", 3)], ROW_JOIN)
    close = join([couple, swap(couple, "col", 3)])
    quad = join([pair, swap(pair, "row", 5)], ROW_JOIN)
    close, blocks = lax.optimization_barrier((close, tiles))
    pairs = split_tiles(blocks[0, 0])
    row_inputs = [close] + [swap(close, "col", offset) for offset in (4, 8, 12)]
    half = join([quad, swap(quad, "row", 13)], ROW_JOIN)
    col_inputs = [half, swap(half, "row", 1)]

    quarter, half_size = close.shape[0], half.shape[0]
    row_parts = product(False, places, blocks[0, 0], pairs, col_inputs, [quarter] * RING)
    later_places, _ = lax.optimization_barrier((places, row_parts[0]))
    col_parts = product(True, later_places, blocks[0, 0], pairs, row_inputs, [half_size] * 2)

    across = fold([row_parts[0], swap(row_parts[2], "col", 8)], 1)
    close = fold([across[0], swap(row_parts[1], "col", 4), swap(row_parts[3], "col", 12)], 2)
    half = fold([col_parts[0], swap(col_parts[1], "row", 1)], 2, ROW_FOLD)
    quad = fold([half[0], swap(half[1], "row", 13)], 2, ROW_FOLD)
    couple = fold([close[0], swap(close[1], "col", 3)], 2)
    pair = fold([quad[0], swap(quad[1], "row", 5)], 2, ROW_FOLD)
    terms = [couple[0], swap(couple[1], "col", 1), pair[0], swap(pair[1], "row", 3)]
    total = functools.reduce(jnp.add, terms)
    return total.transpose(1, 0, 2).reshape(vector_count, width)


def solution(mesh):
    in_specs = (
        P("row", "col", None, None, None),
        P("row", "col", None),
        P("row", "col", None),
        P("row", "col"),
        P(None, ("row", "col")),
    )
    out_specs = P(None, ("row", "col"))
    return jax.shard_map(body, mesh=mesh, in_specs=in_specs, out_specs=out_specs, check_vma=False)
```

```python
import functools

import jax
import jax.numpy as jnp
from jax import lax
from jax.experimental import pallas as pl
from jax.experimental.pallas import tpu as pltpu
from jax.sharding import PartitionSpec as P

CHUNK = 128
AHEAD = 2
SLIM = 62
TLIM = 24
JOIN = 5 * 10 ** 10
FETCH = True
RING = 4
PIECE = 16
PREP_RING = 8
PLIM = 24
PREP = 3 * 10 ** 10
FETCH_COST = 10 ** 10
ROW_JOIN = JOIN
ROW_FOLD = JOIN
FLOPS = 2 * 10 ** 10
SMEM = pl.BlockSpec(memory_space=pltpu.SMEM)
VMEM = pl.BlockSpec(memory_space=pltpu.VMEM)
ANY = pl.BlockSpec(memory_space=pl.ANY)


def split(value):
    high = value.astype(jnp.bfloat16)
    low = (value - high.astype(jnp.float32)).astype(jnp.bfloat16)
    return high, low


def take(refs, count):
    taken = refs[:count]
    del refs[:count]
    return taken


def product_kernel(flipped, pieces, markers, outputs, *refs):
    refs = list(refs)
    places, tiles = take(refs, 2)
    sources = take(refs, pieces)
    take(refs, markers)
    parts = take(refs, outputs)
    inputs, sums = refs
    slots, _, side = tiles.shape
    vectors = sums.shape[1]
    start = 0
    for source in sources:
        high, low = split(source[...])
        inputs[start:start + source.shape[0]] = jnp.concatenate([high, low], axis=1)
        start += source.shape[0]
    inputs[start] = jnp.zeros_like(inputs[start])
    sums[...] = jnp.zeros_like(sums)

    def step(chunk, carry):
        results = []
        for offset in range(CHUNK):
            slot = chunk * CHUNK + offset
            place = places[slot]
            row, col = place // 128, place % 128
            high, low = split(tiles[slot])
            if flipped:
                value, target, contract = inputs[row], col, 0
            else:
                value, target, contract = inputs[col], row, 1
            pair = jnp.concatenate([high, low], axis=contract)
            result = lax.dot_general(
                jnp.concatenate([value, value], axis=1), pair,
                (((1,), (contract,)), ((), ())), preferred_element_type=jnp.float32,
            )
            results.append((target, result[:vectors] + result[vectors:]))
        for target, result in results:
            sums[target] += result
        return carry

    lax.fori_loop(0, slots // CHUNK, step, 0)
    start = 0
    for part in parts:
        part[...] = sums[start:start + part.shape[0]]
        start += part.shape[0]


def product(flipped, places, tiles, sources, sizes, *markers):
    slots, _, side = tiles.shape
    blocks = sum(source.shape[0] for source in sources)
    vectors = sources[0].shape[1]
    out_shape = [jax.ShapeDtypeStruct((size, vectors, side), jnp.float32) for size in sizes]
    return pl.pallas_call(
        functools.partial(product_kernel, flipped, len(sources), len(markers), len(sizes)),
        out_shape=out_shape,
        in_specs=[SMEM] + [VMEM] * (1 + len(sources) + len(markers)),
        out_specs=[VMEM] * len(out_shape),
        scratch_shapes=[
            pltpu.VMEM((blocks + 8, 2 * vectors, side), jnp.bfloat16),
            pltpu.VMEM((sum(sizes) + 8, vectors, side), jnp.float32),
        ],
        compiler_params=pltpu.CompilerParams(vmem_limit_bytes=TLIM * 1024 * 1024),
        cost_estimate=pl.CostEstimate(flops=FLOPS, bytes_accessed=4 * slots * 128 * 128, transcendentals=0),
    )(places, tiles, *sources, *markers)


def fetch_kernel(value, out):
    out[...] = value[...]


def fetch(value):
    return pl.pallas_call(
        fetch_kernel,
        out_shape=jax.ShapeDtypeStruct(value.shape, value.dtype),
        in_specs=[VMEM],
        out_specs=VMEM,
        compiler_params=pltpu.CompilerParams(vmem_limit_bytes=4 * 1024 * 1024),
        cost_estimate=pl.CostEstimate(flops=FETCH_COST, bytes_accessed=1024, transcendentals=0),
    )(value)


def mark_kernel(value, out):
    out[...] = value[0]


def mark(value):
    return pl.pallas_call(
        mark_kernel,
        out_shape=jax.ShapeDtypeStruct(value.shape[1:], value.dtype),
        in_specs=[VMEM],
        out_specs=VMEM,
        compiler_params=pltpu.CompilerParams(vmem_limit_bytes=4 * 1024 * 1024),
        cost_estimate=pl.CostEstimate(flops=PREP, bytes_accessed=1 << 24, transcendentals=0),
    )(value)


def join_kernel(*refs):
    out = refs[-1]
    start = 0
    for part in refs[:-1]:
        out[start:start + part.shape[0]] = part[...]
        start += part.shape[0]


def join(parts, cost=JOIN):
    size = sum(part.shape[0] for part in parts)
    return pl.pallas_call(
        join_kernel,
        out_shape=jax.ShapeDtypeStruct((size, *parts[0].shape[1:]), parts[0].dtype),
        in_specs=[VMEM] * len(parts),
        out_specs=VMEM,
        compiler_params=pltpu.CompilerParams(vmem_limit_bytes=4 * 1024 * 1024),
        cost_estimate=pl.CostEstimate(flops=cost, bytes_accessed=1024, transcendentals=0),
    )(*parts)


def fold_kernel(count, *refs):
    total = refs[0][...]
    for part in refs[1:count]:
        total = total + part[...]
    start = 0
    for out in refs[count:]:
        out[...] = total[start:start + out.shape[0]]
        start += out.shape[0]


def fold(parts, pieces, cost=JOIN):
    size, *rest = parts[0].shape
    out = jax.ShapeDtypeStruct((size // pieces, *rest), parts[0].dtype)
    return pl.pallas_call(
        functools.partial(fold_kernel, len(parts)),
        out_shape=[out] * pieces,
        in_specs=[VMEM] * len(parts),
        out_specs=[VMEM] * pieces,
        compiler_params=pltpu.CompilerParams(vmem_limit_bytes=4 * 1024 * 1024),
        cost_estimate=pl.CostEstimate(flops=cost, bytes_accessed=1024, transcendentals=0),
    )(*parts)


def body(tiles, tile_rows, tile_cols, tile_counts, vectors):
    vector_count, width = vectors.shape
    slots, side = tiles.shape[2:4]
    local_blocks = width // side
    row_devices = lax.axis_size("row")
    col_devices = lax.axis_size("col")
    own = vectors.reshape(vector_count, local_blocks, side).transpose(1, 0, 2)

    def swap(value, axis, offset):
        return lax.ppermute(value, axis, [(j, j ^ offset) for j in range(lax.axis_size(axis))])

    def gray(offset):
        return offset ^ (offset >> 1)

    rows, cols = tile_rows[0, 0], tile_cols[0, 0]
    row_offset = (rows // local_blocks) ^ lax.axis_index("col")
    col_offset = (cols // local_blocks) ^ lax.axis_index("row")
    row_offset = (row_offset & 12) + gray(row_offset & 3)
    near_z, near_x = col_offset >> 1 & 1, gray(col_offset >> 2)
    other_core = col_offset & 1 ^ near_z ^ near_x & 1 ^ near_x >> 1
    slot = jnp.arange(slots, dtype=jnp.int32)

    def place(col_offset):
        places = (row_offset * local_blocks + rows % local_blocks) * 128 + col_offset * local_blocks + cols % local_blocks
        return jnp.where(slot < tile_counts[0, 0], places, col_devices * local_blocks * 128 + row_devices * local_blocks)

    places = place((near_x >> 1) * 8 + other_core * 4 + (near_x & 1) * 2 + near_z)
    scatter_places = place(other_core * 8 + near_x * 2 + near_z)

    local = fetch(own) if FETCH else own
    couple = join([local, swap(own, "col", 1)])
    pair = join([local, swap(own, "row", 3)], ROW_JOIN)
    close = join([couple, swap(couple, "col", 3)])
    quad = join([pair, swap(pair, "row", 5)], ROW_JOIN)
    marker = mark(close)
    row_inputs = [close] + [swap(close, "col", offset) for offset in (4, 8, 12)]
    half = join([quad, swap(quad, "row", 1)], ROW_JOIN)
    col_inputs = [half, swap(half, "row", 13)]

    quarter, half_size = close.shape[0], half.shape[0]
    row_parts = product(False, places, tiles[0, 0], col_inputs, [quarter] * RING, marker)
    later_places, _ = lax.optimization_barrier((scatter_places, row_parts[0]))
    col_parts = product(True, later_places, tiles[0, 0], row_inputs, [half_size] * 2)

    across = fold([row_parts[0], swap(row_parts[2], "col", 8)], 1)
    close = fold([across[0], swap(row_parts[1], "col", 4), swap(row_parts[3], "col", 12)], 2)
    half = fold([col_parts[0], swap(col_parts[1], "row", 1)], 2, ROW_FOLD)
    quad = fold([half[0], swap(half[1], "row", 13)], 2, ROW_FOLD)
    couple = fold([close[0], swap(close[1], "col", 3)], 2)
    pair = fold([quad[0], swap(quad[1], "row", 5)], 2, ROW_FOLD)
    terms = [couple[0], swap(couple[1], "col", 1), pair[0], swap(pair[1], "row", 3)]
    total = functools.reduce(jnp.add, terms)
    return total.transpose(1, 0, 2).reshape(vector_count, width)


def solution(mesh):
    in_specs = (
        P("row", "col", None, None, None),
        P("row", "col", None),
        P("row", "col", None),
        P("row", "col"),
        P(None, ("row", "col")),
    )
    out_specs = P(None, ("row", "col"))
    return jax.shard_map(body, mesh=mesh, in_specs=in_specs, out_specs=out_specs, check_vma=False)
```

```python
import functools

import jax
import jax.numpy as jnp
from jax import lax
from jax.experimental import pallas as pl
from jax.experimental.pallas import tpu as pltpu
from jax.sharding import PartitionSpec as P

CHUNK = 128
AHEAD = 2
SLIM = 62
TLIM = 24
JOIN = 5 * 10 ** 10
FETCH = True
RING = 4
PIECE = 16
PREP_RING = 8
PLIM = 24
PREP = 3 * 10 ** 10
FETCH_COST = 10 ** 10
ROW_JOIN = JOIN
ROW_FOLD = JOIN
FLOPS = 2 * 10 ** 10
SMEM = pl.BlockSpec(memory_space=pltpu.SMEM)
VMEM = pl.BlockSpec(memory_space=pltpu.VMEM)
ANY = pl.BlockSpec(memory_space=pl.ANY)


def split(value):
    high = value.astype(jnp.bfloat16)
    low = (value - high.astype(jnp.float32)).astype(jnp.bfloat16)
    return high, low


def take(refs, count):
    taken = refs[:count]
    del refs[:count]
    return taken


def product_kernel(flipped, pieces, markers, outputs, *refs):
    refs = list(refs)
    places, tiles = take(refs, 2)
    sources = take(refs, pieces)
    take(refs, markers)
    parts = take(refs, outputs)
    inputs, sums = refs
    slots, _, side = tiles.shape
    vectors = sums.shape[1]
    start = 0
    for source in sources:
        high, low = split(source[...])
        inputs[start:start + source.shape[0]] = jnp.concatenate([high, low], axis=1)
        start += source.shape[0]
    inputs[start] = jnp.zeros_like(inputs[start])
    sums[...] = jnp.zeros_like(sums)

    def step(chunk, carry):
        results = []
        for offset in range(CHUNK):
            slot = chunk * CHUNK + offset
            place = places[slot]
            row, col = place // 128, place % 128
            high, low = split(tiles[slot])
            if flipped:
                value, target, contract = inputs[row], col, 0
            else:
                value, target, contract = inputs[col], row, 1
            pair = jnp.concatenate([high, low], axis=contract)
            result = lax.dot_general(
                jnp.concatenate([value, value], axis=1), pair,
                (((1,), (contract,)), ((), ())), preferred_element_type=jnp.float32,
            )
            results.append((target, result[:vectors] + result[vectors:]))
        for target, result in results:
            sums[target] += result
        return carry

    lax.fori_loop(0, slots // CHUNK, step, 0)
    start = 0
    for part in parts:
        part[...] = sums[start:start + part.shape[0]]
        start += part.shape[0]


def product(flipped, places, tiles, sources, sizes, *markers):
    slots, _, side = tiles.shape
    blocks = sum(source.shape[0] for source in sources)
    vectors = sources[0].shape[1]
    out_shape = [jax.ShapeDtypeStruct((size, vectors, side), jnp.float32) for size in sizes]
    return pl.pallas_call(
        functools.partial(product_kernel, flipped, len(sources), len(markers), len(sizes)),
        out_shape=out_shape,
        in_specs=[SMEM] + [VMEM] * (1 + len(sources) + len(markers)),
        out_specs=[VMEM] * len(out_shape),
        scratch_shapes=[
            pltpu.VMEM((blocks + 8, 2 * vectors, side), jnp.bfloat16),
            pltpu.VMEM((sum(sizes) + 8, vectors, side), jnp.float32),
        ],
        compiler_params=pltpu.CompilerParams(vmem_limit_bytes=TLIM * 1024 * 1024),
        cost_estimate=pl.CostEstimate(flops=FLOPS, bytes_accessed=4 * slots * 128 * 128, transcendentals=0),
    )(places, tiles, *sources, *markers)


def fetch_kernel(value, out):
    out[...] = value[...]


def fetch(value):
    return pl.pallas_call(
        fetch_kernel,
        out_shape=jax.ShapeDtypeStruct(value.shape, value.dtype),
        in_specs=[VMEM],
        out_specs=VMEM,
        compiler_params=pltpu.CompilerParams(vmem_limit_bytes=4 * 1024 * 1024),
        cost_estimate=pl.CostEstimate(flops=FETCH_COST, bytes_accessed=1024, transcendentals=0),
    )(value)


def mark_kernel(value, out):
    out[...] = value[0]


def mark(value):
    return pl.pallas_call(
        mark_kernel,
        out_shape=jax.ShapeDtypeStruct(value.shape[1:], value.dtype),
        in_specs=[VMEM],
        out_specs=VMEM,
        compiler_params=pltpu.CompilerParams(vmem_limit_bytes=4 * 1024 * 1024),
        cost_estimate=pl.CostEstimate(flops=PREP, bytes_accessed=1 << 24, transcendentals=0),
    )(value)


def join_kernel(*refs):
    out = refs[-1]
    start = 0
    for part in refs[:-1]:
        out[start:start + part.shape[0]] = part[...]
        start += part.shape[0]


def join(parts, cost=JOIN):
    size = sum(part.shape[0] for part in parts)
    return pl.pallas_call(
        join_kernel,
        out_shape=jax.ShapeDtypeStruct((size, *parts[0].shape[1:]), parts[0].dtype),
        in_specs=[VMEM] * len(parts),
        out_specs=VMEM,
        compiler_params=pltpu.CompilerParams(vmem_limit_bytes=4 * 1024 * 1024),
        cost_estimate=pl.CostEstimate(flops=cost, bytes_accessed=1024, transcendentals=0),
    )(*parts)


def fold_kernel(count, *refs):
    total = refs[0][...]
    for part in refs[1:count]:
        total = total + part[...]
    start = 0
    for out in refs[count:]:
        out[...] = total[start:start + out.shape[0]]
        start += out.shape[0]


def fold(parts, pieces, cost=JOIN):
    size, *rest = parts[0].shape
    out = jax.ShapeDtypeStruct((size // pieces, *rest), parts[0].dtype)
    return pl.pallas_call(
        functools.partial(fold_kernel, len(parts)),
        out_shape=[out] * pieces,
        in_specs=[VMEM] * len(parts),
        out_specs=[VMEM] * pieces,
        compiler_params=pltpu.CompilerParams(vmem_limit_bytes=4 * 1024 * 1024),
        cost_estimate=pl.CostEstimate(flops=cost, bytes_accessed=1024, transcendentals=0),
    )(*parts)


def finish_kernel(*refs):
    out = refs[-1]
    total = refs[0][...]
    for part in refs[1:-1]:
        total = total + part[...]
    blocks, _, side = total.shape
    for block in range(blocks):
        out[:, block * side:(block + 1) * side] = total[block]


def finish(terms, like):
    return pl.pallas_call(
        finish_kernel,
        out_shape=jax.ShapeDtypeStruct(like.shape, like.dtype),
        in_specs=[VMEM] * len(terms),
        out_specs=VMEM,
        compiler_params=pltpu.CompilerParams(vmem_limit_bytes=4 * 1024 * 1024),
    )(*terms)


def body(tiles, tile_rows, tile_cols, tile_counts, vectors):
    vector_count, width = vectors.shape
    slots, side = tiles.shape[2:4]
    local_blocks = width // side
    row_devices = lax.axis_size("row")
    col_devices = lax.axis_size("col")
    own = vectors.reshape(vector_count, local_blocks, side).transpose(1, 0, 2)

    def swap(value, axis, offset):
        return lax.ppermute(value, axis, [(j, j ^ offset) for j in range(lax.axis_size(axis))])

    def gray(offset):
        return offset ^ (offset >> 1)

    rows, cols = tile_rows[0, 0], tile_cols[0, 0]
    row_offset = (rows // local_blocks) ^ lax.axis_index("col")
    col_offset = (cols // local_blocks) ^ lax.axis_index("row")
    row_offset = (row_offset & 12) + gray(row_offset & 3)
    near_z, near_x = col_offset >> 1 & 1, gray(col_offset >> 2)
    other_core = col_offset & 1 ^ near_z ^ near_x & 1 ^ near_x >> 1
    slot = jnp.arange(slots, dtype=jnp.int32)

    def place(col_offset):
        places = (row_offset * local_blocks + rows % local_blocks) * 128 + col_offset * local_blocks + cols % local_blocks
        return jnp.where(slot < tile_counts[0, 0], places, col_devices * local_blocks * 128 + row_devices * local_blocks)

    places = place((near_x >> 1) * 8 + other_core * 4 + (near_x & 1) * 2 + near_z)
    scatter_places = place(other_core * 8 + near_x * 2 + near_z)

    local = fetch(own) if FETCH else own
    couple = join([local, swap(own, "col", 1)])
    pair = join([local, swap(own, "row", 3)], ROW_JOIN)
    close = join([couple, swap(couple, "col", 3)])
    quad = join([pair, swap(pair, "row", 5)], ROW_JOIN)
    marker = mark(close)
    row_inputs = [close] + [swap(close, "col", offset) for offset in (4, 8, 12)]
    half = join([quad, swap(quad, "row", 1)], ROW_JOIN)
    col_inputs = [half, swap(half, "row", 13)]

    quarter, half_size = close.shape[0], half.shape[0]
    row_parts = product(False, places, tiles[0, 0], col_inputs, [quarter] * RING, marker)
    later_places, _ = lax.optimization_barrier((scatter_places, row_parts[0]))
    col_parts = product(True, later_places, tiles[0, 0], row_inputs, [half_size] * 2)

    across = fold([row_parts[0], swap(row_parts[2], "col", 8)], 1)
    close = fold([across[0], swap(row_parts[1], "col", 4), swap(row_parts[3], "col", 12)], 2)
    half = fold([col_parts[0], swap(col_parts[1], "row", 1)], 2, ROW_FOLD)
    quad = fold([half[0], swap(half[1], "row", 13)], 2, ROW_FOLD)
    couple = fold([close[0], swap(close[1], "col", 3)], 2)
    pair = fold([quad[0], swap(quad[1], "row", 5)], 2, ROW_FOLD)
    terms = [couple[0], swap(couple[1], "col", 1), pair[0], swap(pair[1], "row", 3)]
    return finish(terms, vectors)


def solution(mesh):
    in_specs = (
        P("row", "col", None, None, None),
        P("row", "col", None),
        P("row", "col", None),
        P("row", "col"),
        P(None, ("row", "col")),
    )
    out_specs = P(None, ("row", "col"))
    return jax.shard_map(body, mesh=mesh, in_specs=in_specs, out_specs=out_specs, check_vma=False)
```
